128 devices in a mesh: grp: 2 (over x_lo), ctx: 64 (over x_hi, y, z, core).
Axes of the slice: x: 4 (x_hi: 2, x_lo: 2; x = x_hi * 2 + x_lo), y: 4, z: 4, core: 2. Of those that a mesh axis runs over, the one named last changes fastest.
Arguments:
- queries: bfloat16 [12288, 1536], P('ctx', 'grp'), may hold values from -9 to 9
- key_tokens: bfloat16 [12288, 1536], P('ctx', 'grp'), may hold values from -9 to 9
- value_tokens: bfloat16 [12288, 1536], P('ctx', 'grp'), may hold values from -6 to 6
- hidden: bfloat16 [12288, 1536], P('ctx'), may hold values from -6 to 6
- out_weight: bfloat16 [1536, 1536], replicated, may hold values from -0.15625 to 0.15625
- attn_gate: float32 [1536], replicated, may hold values from 0.5 to 2
Outputs:
- block_out: bfloat16 [12288, 1536], P('ctx')
The draws below stay inside these ranges and needn't reach their ends.
All inputs are finite; a program needn't handle non-finite values.
Results may differ from the reference program's by a relative error of at most 0.009.
Values may be sent and summed in bfloat16 or wider, within the bound.
A program may use at most 192 MiB of HBM per device.

```python
import jax
import jax.numpy as jnp
from jax import lax

D = 1536
HEADS = 12
DH = 128
HD = 1536
TOK_DEV = 192
SEQ = 12288


def draw_queries(key, part):
    key = jax.random.fold_in(key, 11)
    drawn = jnp.clip(1.8 * jax.random.normal(key, (SEQ, HD), jnp.float32), -5.4, 5.4)
    return drawn.astype(jnp.bfloat16)


def draw_key_tokens(key, part):
    key = jax.random.fold_in(key, 23)
    drawn = jnp.clip(1.8 * jax.random.normal(key, (SEQ, HD), jnp.float32), -5.4, 5.4)
    return drawn.astype(jnp.bfloat16)


def shard_levels(own_key, dims, shards, smallest, top_value):
    factor_of = 1.0
    for axis_at, shards_of in shards:
        draws = jax.random.uniform(jax.random.fold_in(jax.random.fold_in(own_key, 6), axis_at), (shards_of,), jnp.float32, smallest / len(shards), top_value / len(shards))
        factor_of = factor_of * jnp.repeat(jnp.exp(draws), dims[axis_at] // shards_of).reshape((-1,) + (1,) * (len(dims) - 1 - axis_at))
    return factor_of


def normal_values(key, shape, spread, limit, shards=(), kind=jnp.bfloat16):
    array = spread * jax.random.normal(key, shape, jnp.float32)
    if shards:
        array = array * shard_levels(key, shape, shards, -0.22, 0.18)
    return jnp.clip(array, -limit, limit).astype(kind)


def setup_inputs(seed: int = 0) -> dict:
    streams_of = jax.random.split(jax.random.key(seed), 7)
    return {
        "queries": draw_queries(jax.random.fold_in(streams_of[6], 71), 0),
        "key_tokens": draw_key_tokens(jax.random.fold_in(streams_of[6], 71), 0),
        "value_tokens": normal_values(streams_of[2], (SEQ, HD), 1.0, 6.0, ((0, 64), (1, 2))),
        "hidden": normal_values(streams_of[3], (SEQ, D), 1.0, 6.0, ((0, 64),)),
        "out_weight": normal_values(streams_of[4], (HD, D), HD ** -0.5, 0.15625),
        "attn_gate": jnp.clip(jax.random.uniform(streams_of[5], (D,), jnp.float32, 0.5, 2.0), 0.5, 2.0),
    }


def reference(queries, key_tokens, value_tokens, hidden, out_weight, attn_gate):
    block_rows = TOK_DEV * 4
    count = SEQ // block_rows
    key_heads = key_tokens.reshape(SEQ, HEADS, DH).astype(jnp.float32)
    value_heads = value_tokens.reshape(SEQ, HEADS, DH).astype(jnp.float32)
    blocks = queries.reshape(count, block_rows, HEADS, DH)

    def one_block(query_block):
        scores = jnp.einsum("thd,shd->hts", query_block.astype(jnp.float32), key_heads) * (DH ** -0.5)
        row_max = jnp.max(scores, axis=-1)
        weights = jnp.exp(scores - row_max[:, :, None])
        mass = jnp.sum(weights, axis=-1)
        rounded = lax.optimization_barrier(weights.astype(jnp.bfloat16)).astype(jnp.float32)
        mixed = jnp.einsum("hts,shd->thd", rounded, value_heads)
        return (mixed / jnp.transpose(mass)[:, :, None]).reshape(block_rows, HEADS * DH)

    attended = lax.map(one_block, blocks).reshape(SEQ, HEADS * DH).astype(jnp.bfloat16)
    projected = jnp.dot(attended, out_weight, preferred_element_type=jnp.float32)
    return (hidden.astype(jnp.float32) + attn_gate * projected).astype(jnp.bfloat16)
```

```python
import jax
import jax.numpy as jnp
from jax import lax
from jax.experimental import pallas as pl
from jax.experimental.pallas import tpu as pltpu
from jax.sharding import PartitionSpec as P

DH = 128
TOK = 192
HEADS_DEV = 3
RING = 4
SCALE = DH**-0.5 * 1.4426950408889634
NT = (((1,), (1,)), ((), ()))
NN = (((1,), (0,)), ((), ()))
MESH = pl.DeviceIdType.MESH
KV_AXIS = ("y", "z", "y")
Q_AXIS = ("z", "y", "z")
PAIRS = ((1, 3), (2, 0))


def kernel(
    q_in, k_in, v_in, hidden_in, w_in, gate_ref, out_ref,
    kv, qb, o_send, o_recv, s_send, s_recv, att, a_send, w_buf, hid_buf,
    loc_sem, big_sem, x_send, x_recv, kv_send, kv_recv, q_send, q_recv,
    f_send, f_recv, o_ssem, o_rsem, s_ssem, s_rsem, a_ssem, a_rsem,
):
    g = lax.axis_index("grp")
    t = lax.axis_index("ctx")
    core = t % 2
    place = {"xh": t // 32, "y": (t // 8) % 4, "z": (t // 2) % 4, "core": core}
    xh = place["xh"]

    def device(grp=None, **moved):
        at = dict(place, **moved)
        ctx = ((at["xh"] * 4 + at["y"]) * 4 + at["z"]) * 2 + at["core"]
        return (g if grp is None else grp, ctx)

    def ring(axis, step):
        return device(**{axis: (place[axis] + step) % RING})

    sibling = device(core=1 - core)
    x_partner = device(xh=1 - xh)
    x_kinds = (device(grp=1 - g), x_partner, device(grp=1 - g, xh=1 - xh))

    def columns(half, h):
        return pl.ds(pl.multiple_of((half * HEADS_DEV + h) * DH, DH), DH)

    def remote(src, dst, send, recv, to):
        return pltpu.make_async_remote_copy(
            src_ref=src, dst_ref=dst, send_sem=send, recv_sem=recv, device_id=to, device_id_type=MESH
        )

    own = []
    for h in range(HEADS_DEV):
        cols = columns(xh, h)
        own.append((
            pltpu.make_async_copy(k_in.at[:, cols], kv.at[h, 0, 0, 0, :, pl.ds(0, DH)], loc_sem.at[h, 0]),
            pltpu.make_async_copy(v_in.at[:, cols], kv.at[h, 0, 0, 0, :, pl.ds(DH, DH)], loc_sem.at[h, 1]),
            pltpu.make_async_copy(q_in.at[:, cols], qb.at[h, 0, 0], loc_sem.at[h, 2]),
        ))
        for copy in own[h]:
            copy.start()
    w_copy = pltpu.make_async_copy(w_in, w_buf, big_sem.at[0])
    hid_copy = pltpu.make_async_copy(hidden_in, hid_buf, big_sem.at[1])
    w_copy.start()
    hid_copy.start()

    barrier = pltpu.get_barrier_semaphore()
    peers = [ring(a, s) for a in ("y", "z") for s in (1, 2, 3)] + [sibling, *x_kinds]
    for peer in peers:
        pl.semaphore_signal(barrier, inc=1, device_id=peer, device_id_type=MESH)
    pl.semaphore_wait(barrier, len(peers))

    sent = []

    def start(copy):
        copy.start()
        sent.append(copy)

    def x_copies(h):
        cols = columns(1 - xh, h)
        return [
            remote(k_in.at[:, cols], kv.at[h, 0, 1, 0, :, pl.ds(0, DH)], x_send.at[h, 0], x_recv.at[h, 0], x_partner),
            remote(v_in.at[:, cols], kv.at[h, 0, 1, 0, :, pl.ds(DH, DH)], x_send.at[h, 1], x_recv.at[h, 1], x_partner),
            remote(q_in.at[:, cols], qb.at[h, 0, 1], x_send.at[h, 2], x_recv.at[h, 2], x_partner),
        ]

    def kv_copy(h, xr, step):
        slot = RING - step
        return remote(
            kv.at[h, 0, xr, 0], kv.at[h, 0, xr, slot],
            kv_send.at[h, xr, slot - 1], kv_recv.at[h, xr, slot - 1], ring(KV_AXIS[h], step),
        )

    def q_copy(h, xr, step):
        slot = RING - step
        return remote(
            qb.at[h, 0, xr], qb.at[h, slot, xr],
            q_send.at[h, xr, slot - 1], q_recv.at[h, xr, slot - 1], ring(Q_AXIS[h], step),
        )

    def push(h, xr):
        for step in (2, 1, 3):
            start(kv_copy(h, xr, step))
        for step in (2, 1, 3):
            start(q_copy(h, xr, step))

    def forward_copy(h, xr):
        return remote(kv.at[h, 0, xr], kv.at[h, 1, xr], f_send.at[h, xr], f_recv.at[h, xr], sibling)

    for h in range(HEADS_DEV):
        for copy in x_copies(h):
            start(copy)
        for copy in own[h]:
            copy.wait()
        push(h, 0)
    for h in range(HEADS_DEV):
        for copy in x_copies(h):
            copy.wait_recv()
        push(h, 1)

    def gathered(h):
        for xr in range(2):
            for step in (1, 2, 3):
                kv_copy(h, xr, step).wait_recv()
            start(forward_copy(h, xr))
        for xr in range(2):
            for step in (1, 2, 3):
                q_copy(h, xr, step).wait_recv()

    def o_copies(h, d):
        slot = RING - d
        to = ring(Q_AXIS[h], d)
        return (
            remote(o_send.at[h, d], o_recv.at[h, slot - 1], o_ssem.at[h, slot - 1], o_rsem.at[h, slot - 1], to),
            remote(s_send.at[h, d], s_recv.at[h, slot - 1], s_ssem.at[h, slot - 1], s_rsem.at[h, slot - 1], to),
        )

    def attend(h, ds):
        blocks = [(cs, xr) for cs in range(2) for xr in range(2)]
        items = [(d, b) for d in ds for b in blocks]
        stacked = {}
        for d in ds:
            scaled = qb[h, d].reshape(2 * TOK, DH).astype(jnp.float32) * SCALE
            high = scaled.astype(jnp.bfloat16)
            low = (scaled - high.astype(jnp.float32)).astype(jnp.bfloat16)
            stacked[d] = jnp.concatenate([high, low], axis=1)

        def scores(item):
            d, (cs, xr) = item
            keys = kv[h, cs, xr, :, :, :DH].reshape(RING * TOK, DH)
            return lax.dot_general(
                stacked[d], jnp.concatenate([keys, keys], axis=1), NT, preferred_element_type=jnp.float32
            )

        state = {}
        ahead = scores(items[0])
        for n, (d, (cs, xr)) in enumerate(items):
            now = ahead
            if n + 1 < len(items):
                ahead = scores(items[n + 1])
            values = kv[h, cs, xr, :, :, DH:].reshape(RING * TOK, DH)
            top = jnp.max(now, axis=1, keepdims=True)
            if d in state:
                top = jnp.maximum(top, state[d][0])
            weights = jnp.exp2(now - top).astype(jnp.bfloat16)
            mixed = lax.dot_general(
                weights, jnp.concatenate([values, jnp.ones_like(values)], axis=1), NN,
                preferred_element_type=jnp.float32,
            )
            if d in state:
                mixed = mixed + state[d][1] * jnp.exp2(state[d][0] - top)
            state[d] = (top, mixed)
        for d in ds:
            top, mixed = state[d]
            mass = mixed[:, DH:]
            o_send[h, d] = (mixed[:, :DH] / mass).astype(jnp.bfloat16)
            s_send[h, d] = jnp.transpose(top + jnp.log2(mass))[:8]
        for d in ds:
            if d:
                for copy in o_copies(h, d):
                    start(copy)

    def a_copies(h):
        at = (g * 2 + xh) * HEADS_DEV + h
        return [
            remote(att.at[at] if kind == 0 else a_send.at[h], att.at[at], a_ssem.at[h, kind], a_rsem.at[h, kind], x_kinds[kind])
            for kind in range(3)
        ]

    def a_arrivals(h):
        places = ((1 - g) * 2 + xh, g * 2 + 1 - xh, (1 - g) * 2 + 1 - xh)
        return [
            remote(a_send.at[h], att.at[places[kind] * HEADS_DEV + h], a_ssem.at[h, kind], a_rsem.at[h, kind], x_kinds[kind])
            for kind in range(3)
        ]

    def combine(h):
        for d in (1, 2, 3):
            for copy in o_copies(h, d):
                copy.wait_recv()
        sums = [s_send[h, 0]] + [s_recv[h, j] for j in range(3)]
        parts = [o_send[h, 0]] + [o_recv[h, j] for j in range(3)]
        top = jnp.maximum(jnp.maximum(sums[0], sums[1]), jnp.maximum(sums[2], sums[3]))
        shares = [jnp.exp2(s - top) for s in sums]
        total = (shares[0] + shares[1]) + (shares[2] + shares[3])
        whole = None
        for share, part in zip(shares, parts):
            by_row = jnp.transpose(jnp.broadcast_to((share / total)[:1], (DH, 2 * TOK)))
            term = by_row * part.astype(jnp.float32)
            whole = term if whole is None else whole + term
        whole = whole.astype(jnp.bfloat16)
        att[(g * 2 + xh) * HEADS_DEV + h] = whole[:TOK]
        a_send[h] = whole[TOK:]
        for copy in a_copies(h):
            start(copy)

    for h in range(HEADS_DEV):
        gathered(h)
        for xr in range(2):
            forward_copy(h, xr).wait_recv()
        for ds in PAIRS:
            attend(h, ds)
        if h:
            combine(h - 1)
    combine(HEADS_DEV - 1)

    w_copy.wait()
    hid_copy.wait()
    for h in range(HEADS_DEV):
        for copy in a_arrivals(h):
            copy.wait_recv()
    pairs = [jnp.concatenate([att[2 * i], att[2 * i + 1]], axis=1) for i in range(6)]
    rows = jnp.concatenate(pairs, axis=1)

    def project(j, carry):
        cols = pl.ds(pl.multiple_of(j * 256, 256), 256)
        projected = jnp.dot(rows, w_buf[:, cols], preferred_element_type=jnp.float32)
        out_ref[:, cols] = (hid_buf[:, cols].astype(jnp.float32) + gate_ref[:, cols] * projected).astype(jnp.bfloat16)
        return carry

    lax.fori_loop(0, 6, project, 0)
    for copy in sent:
        copy.wait_send()


def on_device(queries, key_tokens, value_tokens, hidden, out_weight, attn_gate):
    bf16, f32 = jnp.bfloat16, jnp.float32
    dma = pltpu.SemaphoreType.DMA
    anywhere = pl.BlockSpec(memory_space=pl.ANY)
    in_vmem = pl.BlockSpec(memory_space=pltpu.VMEM)
    n = HEADS_DEV
    return pl.pallas_call(
        kernel,
        out_shape=jax.ShapeDtypeStruct(hidden.shape, bf16),
        in_specs=[anywhere] * 5 + [in_vmem],
        out_specs=in_vmem,
        scratch_shapes=[
            pltpu.VMEM((n, 2, 2, RING, TOK, 2 * DH), bf16),
            pltpu.VMEM((n, RING, 2, TOK, DH), bf16),
            pltpu.VMEM((n, RING, 2 * TOK, DH), bf16),
            pltpu.VMEM((n, RING - 1, 2 * TOK, DH), bf16),
            pltpu.VMEM((n, RING, 8, 2 * TOK), f32),
            pltpu.VMEM((n, RING - 1, 8, 2 * TOK), f32),
            pltpu.VMEM((4 * n, TOK, DH), bf16),
            pltpu.VMEM((n, TOK, DH), bf16),
            pltpu.VMEM(out_weight.shape, bf16),
            pltpu.VMEM(hidden.shape, bf16),
            dma((n, 3)), dma((2,)), dma((n, 3)), dma((n, 3)),
            dma((n, 2, 3)), dma((n, 2, 3)), dma((n, 2, 3)), dma((n, 2, 3)),
            dma((n, 2)), dma((n, 2)), dma((n, 3)), dma((n, 3)), dma((n, 3)), dma((n, 3)),
            dma((n, 3)), dma((n, 3)),
        ],
        compiler_params=pltpu.CompilerParams(
            collective_id=0, has_side_effects=True, vmem_limit_bytes=56 << 20
        ),
        cost_estimate=pl.CostEstimate(flops=15_000_000_000, bytes_accessed=8_000_000, transcendentals=14_000_000),
    )(queries, key_tokens, value_tokens, hidden, out_weight, attn_gate.reshape(1, -1))


def solution(mesh):
    return jax.shard_map(
        on_device,
        mesh=mesh,
        in_specs=(P("ctx", "grp"), P("ctx", "grp"), P("ctx", "grp"), P("ctx", None), P(), P()),
        out_specs=P("ctx", None),
        check_vma=False,
    )
```

```python
import jax
import jax.numpy as jnp
from jax import lax
from jax.experimental import pallas as pl
from jax.experimental.pallas import tpu as pltpu
from jax.sharding import PartitionSpec as P

DH = 128
TOK = 192
HEADS_DEV = 3
RING = 4
SCALE = DH**-0.5 * 1.4426950408889634
NT = (((1,), (1,)), ((), ()))
NN = (((1,), (0,)), ((), ()))
MESH = pl.DeviceIdType.MESH
KV_AXIS = ("y", "z", "z")
Q_AXIS = ("z", "y", "y")
RELAYED = (False, True, True)
HALF = TOK // 2


def kernel(
    q_in, k_in, v_in, hidden_in, w_in, gate_in, out_hbm,
    kv, qb, o_send, o_recv, s_send, s_recv, att, a_send, w_buf, hid_buf, proj, top_buf, mix_buf, gate_ref, out_ref, x_kv_buf, x_q_buf,
    loc_sem, stage_sem, big_sem, x_send, x_recv, kv_send, kv_recv, q_send, q_recv,
    f_send, f_recv, r_send, r_recv, o_ssem, o_rsem, s_ssem, s_rsem, a_ssem, a_rsem,
):
    g = lax.axis_index("grp")
    t = lax.axis_index("ctx")
    core = t % 2
    place = {"xh": t // 32, "y": (t // 8) % 4, "z": (t // 2) % 4, "core": core}
    xh = place["xh"]

    def device(grp=None, **moved):
        at = dict(place, **moved)
        ctx = ((at["xh"] * 4 + at["y"]) * 4 + at["z"]) * 2 + at["core"]
        return (g if grp is None else grp, ctx)

    def ring(axis, step):
        return device(**{axis: (place[axis] + step) % RING})

    sibling = device(core=1 - core)
    x_partner = device(xh=1 - xh)
    x_kinds = (device(grp=1 - g), x_partner, device(grp=1 - g, xh=1 - xh))

    def columns(half, h):
        return pl.ds(pl.multiple_of((half * HEADS_DEV + h) * DH, DH), DH)

    def remote(src, dst, send, recv, to):
        return pltpu.make_async_remote_copy(
            src_ref=src, dst_ref=dst, send_sem=send, recv_sem=recv, device_id=to, device_id_type=MESH
        )

    own, stage = [], []
    for h in range(HEADS_DEV):
        cols = columns(xh, h)
        own.append((
            pltpu.make_async_copy(k_in.at[:, cols], kv.at[h, 0, 0, 0, :, pl.ds(0, DH)], loc_sem.at[h, 0]),
            pltpu.make_async_copy(v_in.at[:, cols], kv.at[h, 0, 0, 0, :, pl.ds(DH, DH)], loc_sem.at[h, 1]),
            pltpu.make_async_copy(q_in.at[:, cols], qb.at[h, 0, 0], loc_sem.at[h, 2]),
        ))
        cols = columns(1 - xh, h)
        stage.append((
            pltpu.make_async_copy(k_in.at[:, cols], x_kv_buf.at[h, :, pl.ds(0, DH)], stage_sem.at[h, 0]),
            pltpu.make_async_copy(v_in.at[:, cols], x_kv_buf.at[h, :, pl.ds(DH, DH)], stage_sem.at[h, 1]),
            pltpu.make_async_copy(q_in.at[:, cols], x_q_buf.at[h], stage_sem.at[h, 2]),
        ))
        for copy in (*stage[h], *own[h]):
            copy.start()
    w_copy = pltpu.make_async_copy(w_in, w_buf, big_sem.at[0])
    hid_copy = pltpu.make_async_copy(hidden_in, hid_buf, big_sem.at[1])
    gate_copy = pltpu.make_async_copy(gate_in, gate_ref, big_sem.at[2])

    barrier = pltpu.get_barrier_semaphore()
    peers = [ring(a, s) for a in ("y", "z") for s in (1, 2, 3)] + [sibling, *x_kinds]
    for peer in peers:
        pl.semaphore_signal(barrier, inc=1, device_id=peer, device_id_type=MESH)
    pl.semaphore_wait(barrier, len(peers))

    sent = []

    def start(copy):
        copy.start()
        sent.append(copy)

    def x_query(h):
        return remote(x_q_buf.at[h], qb.at[h, 0, 1], x_send.at[h, 0], x_recv.at[h, 0], x_partner)

    def x_kv(h):
        return remote(x_kv_buf.at[h], kv.at[h, 0, 1, 0], x_send.at[h, 1], x_recv.at[h, 1], x_partner)

    def kv_copy(h, xr, step):
        slot = RING - step
        return remote(
            kv.at[h, 0, xr, 0], kv.at[h, 0, xr, slot],
            kv_send.at[h, xr, slot - 1], kv_recv.at[h, xr, slot - 1], ring(KV_AXIS[h], step),
        )

    def q_copy(h, xr, step):
        slot = RING - step
        return remote(
            qb.at[h, 0, xr], qb.at[h, slot, xr],
            q_send.at[h, xr, slot - 1], q_recv.at[h, xr, slot - 1], ring(Q_AXIS[h], step),
        )

    def push_queries(h, xr):
        for step in (2, 1, 3):
            start(q_copy(h, xr, step))

    def push_kv(h, xr):
        for step in (1, 3) if RELAYED[h] else (2, 1, 3):
            start(kv_copy(h, xr, step))

    def relay_copy(h, xr, step):
        slot = RING - step
        rows = pl.ds(0 if step == 1 else HALF, HALF)
        n = 0 if step == 1 else 1
        return remote(
            kv.at[h, 0, xr, slot, rows], kv.at[h, 0, xr, 2, rows],
            r_send.at[h, xr, n], r_recv.at[h, xr, n], ring(KV_AXIS[h], step),
        )

    def relay(h, xr):
        for step in (1, 3):
            kv_copy(h, xr, step).wait_recv()
            start(relay_copy(h, xr, step))

    def forward_copy(h, xr):
        return remote(kv.at[h, 0, xr], kv.at[h, 1, xr], f_send.at[h, xr], f_recv.at[h, xr], sibling)

    def gathered(h, xr):
        if RELAYED[h]:
            for step in (1, 3):
                relay_copy(h, xr, step).wait_recv()
        else:
            for step in (1, 2, 3):
                kv_copy(h, xr, step).wait_recv()
        start(forward_copy(h, xr))

    def ready(h, xr):
        forward_copy(h, xr).wait_recv()

    def queries_ready(h):
        for xr in range(2):
            for step in (1, 2, 3):
                q_copy(h, xr, step).wait_recv()

    def o_copies(h, d):
        slot = RING - d
        to = ring(Q_AXIS[h], d)
        return (
            remote(o_send.at[h, d], o_recv.at[h, slot - 1], o_ssem.at[h, slot - 1], o_rsem.at[h, slot - 1], to),
            remote(s_send.at[h, d], s_recv.at[h, slot - 1], s_ssem.at[h, slot - 1], s_rsem.at[h, slot - 1], to),
        )

    def attend(rows, blocks, begin=True, end=True):
        items = [(row, block) for row in rows for block in blocks]
        stacked = {}
        for h, d in rows:
            scaled = qb[h, d].reshape(2 * TOK, DH).astype(jnp.float32) * SCALE
            high = scaled.astype(jnp.bfloat16)
            low = (scaled - high.astype(jnp.float32)).astype(jnp.bfloat16)
            stacked[h, d] = jnp.concatenate([high, low], axis=1)

        def scores(item):
            row, (cs, xr) = item
            keys = kv[row[0], cs, xr, :, :, :DH].reshape(RING * TOK, DH)
            return lax.dot_general(
                stacked[row], jnp.concatenate([keys, keys], axis=1), NT, preferred_element_type=jnp.float32
            )

        state = {}
        if not begin:
            for h, d in rows:
                state[h, d] = (top_buf[h, d - 1], mix_buf[h, d - 1])
        ahead = scores(items[0])
        for n, (row, (cs, xr)) in enumerate(items):
            now = ahead
            if n + 1 < len(items):
                ahead = scores(items[n + 1])
            values = kv[row[0], cs, xr, :, :, DH:].reshape(RING * TOK, DH)
            top = jnp.max(now, axis=1, keepdims=True)
            if row in state:
                top = jnp.maximum(top, state[row][0])
            weights = jnp.exp2(now - top).astype(jnp.bfloat16)
            mixed = lax.dot_general(
                weights, jnp.concatenate([values, jnp.ones_like(values)], axis=1), NN,
                preferred_element_type=jnp.float32,
            )
            if row in state:
                mixed = mixed + state[row][1] * jnp.exp2(state[row][0] - top)
            state[row] = (top, mixed)
        for h, d in rows:
            top, mixed = state[h, d]
            if end:
                mass = mixed[:, DH:]
                o_send[h, d] = (mixed[:, :DH] / mass).astype(jnp.bfloat16)
                s_send[h, d] = jnp.transpose(top + jnp.log2(mass))[:8]
            else:
                top_buf[h, d - 1] = top
                mix_buf[h, d - 1] = mixed
        for h, d in rows:
            if end and d:
                for copy in o_copies(h, d):
                    start(copy)

    def a_copies(h):
        at = (g * 2 + xh) * HEADS_DEV + h
        return [
            remote(att.at[at] if kind == 0 else a_send.at[h], att.at[at], a_ssem.at[h, kind], a_rsem.at[h, kind], x_kinds[kind])
            for kind in range(3)
        ]

    def a_arrivals(h):
        places = ((1 - g) * 2 + xh, g * 2 + 1 - xh, (1 - g) * 2 + 1 - xh)
        return [
            remote(a_send.at[h], att.at[places[kind] * HEADS_DEV + h], a_ssem.at[h, kind], a_rsem.at[h, kind], x_kinds[kind])
            for kind in range(3)
        ]

    def combine(h):
        for d in (1, 2, 3):
            for copy in o_copies(h, d):
                copy.wait_recv()
        sums = [s_send[h, 0]] + [s_recv[h, j] for j in range(3)]
        parts = [o_send[h, 0]] + [o_recv[h, j] for j in range(3)]
        top = jnp.maximum(jnp.maximum(sums[0], sums[1]), jnp.maximum(sums[2], sums[3]))
        shares = [jnp.exp2(s - top) for s in sums]
        total = (shares[0] + shares[1]) + (shares[2] + shares[3])
        whole = None
        for share, part in zip(shares, parts):
            by_row = jnp.transpose(jnp.broadcast_to((share / total)[:1], (DH, 2 * TOK)))
            term = by_row * part.astype(jnp.float32)
            whole = term if whole is None else whole + term
        whole = whole.astype(jnp.bfloat16)
        att[(g * 2 + xh) * HEADS_DEV + h] = whole[:TOK]
        a_send[h] = whole[TOK:]
        for copy in a_copies(h):
            start(copy)

    def project(h, first):
        places = [k * HEADS_DEV + h for k in range(4)]
        rows = jnp.concatenate([att[p] for p in places], axis=1)
        for n in range(0, w_buf.shape[1], 512):
            weight = jnp.concatenate([w_buf[p * DH : (p + 1) * DH, n : n + 512] for p in places], axis=0)
            part = jnp.dot(rows, weight, preferred_element_type=jnp.float32)
            proj[:, n : n + 512] = part if first else proj[:, n : n + 512] + part

    def wait_attended(h):
        for copy in a_arrivals(h):
            copy.wait_recv()

    def remote_rows(h):
        return [(h, d) for d in (1, 3, 2)]

    def start_all(copies):
        for copy in copies:
            start(copy)

    def wait_own(h):
        for copy in own[h]:
            copy.wait()

    def wait_staged(h):
        for copy in stage[h]:
            copy.wait()

    def partner_queries(h):
        x_query(h).wait_recv()
        push_queries(h, 1)

    def partner_kv(h):
        x_kv(h).wait_recv()
        push_kv(h, 1)

    wait_staged(0)
    start(x_query(0))
    wait_own(0)
    push_queries(0, 0)
    push_kv(0, 0)
    wait_staged(1)
    start(x_query(1))
    start(x_kv(0))
    wait_own(1)
    push_kv(1, 0)
    push_queries(1, 0)
    start(x_kv(1))
    wait_staged(2)
    start(x_query(2))
    start(x_kv(2))
    partner_queries(0)
    partner_queries(1)
    partner_kv(0)
    wait_own(2)
    push_kv(2, 0)
    push_queries(2, 0)
    w_copy.start()
    hid_copy.start()
    gate_copy.start()
    relay(1, 0)
    gathered(0, 0)
    queries_ready(0)
    first, second, third = ([(h, d) for d in (1, 3, 2)] for h in range(HEADS_DEV))
    attend(first, [(0, 0)], end=False)
    partner_kv(1)
    ready(0, 0)
    attend(first, [(1, 0)], begin=False, end=False)
    relay(2, 0)
    partner_queries(2)
    partner_kv(2)
    gathered(1, 0)
    queries_ready(1)
    attend(second, [(0, 0)], end=False)
    relay(1, 1)
    ready(1, 0)
    attend(second, [(1, 0)], begin=False, end=False)
    gathered(0, 1)
    attend(first, [(0, 1)], begin=False, end=False)
    relay(2, 1)
    gathered(1, 1)
    ready(0, 1)
    attend(first, [(1, 1)], begin=False)
    gathered(2, 0)
    ready(1, 1)
    attend(second, [(0, 1), (1, 1)], begin=False)
    gathered(2, 1)
    queries_ready(2)
    ready(2, 0)
    attend(third, [(0, 0), (1, 0)], end=False)
    ready(2, 1)
    attend(third, [(0, 1), (1, 1)], begin=False)
    every = [(0, 0), (0, 1), (1, 0), (1, 1)]
    attend([(0, 0), (1, 0)], every)
    combine(0)
    combine(1)
    attend([(2, 0)], every)
    combine(2)
    w_copy.wait()
    hid_copy.wait()
    gate_copy.wait()
    for copy in sent[:-3]:
        copy.wait_send()
    for h in range(HEADS_DEV):
        wait_attended(h)
        project(h, h == 0)
    out_copies = []
    for n in range(2):
        rows = pl.ds(n * HALF, HALF)
        out_ref[rows] = (
            hid_buf[rows].astype(jnp.float32) + gate_ref[...].reshape(1, -1) * proj[rows]
        ).astype(jnp.bfloat16)
        out_copies.append(pltpu.make_async_copy(out_ref.at[rows], out_hbm.at[rows], big_sem.at[3 + n]))
        out_copies[n].start()
    for copy in sent[-3:]:
        copy.wait_send()
    for copy in out_copies:
        copy.wait()


def on_device(queries, key_tokens, value_tokens, hidden, out_weight, attn_gate):
    bf16, f32 = jnp.bfloat16, jnp.float32
    dma = pltpu.SemaphoreType.DMA
    anywhere = pl.BlockSpec(memory_space=pl.ANY)
    n = HEADS_DEV
    return pl.pallas_call(
        kernel,
        out_shape=jax.ShapeDtypeStruct(hidden.shape, bf16),
        in_specs=[anywhere] * 6,
        out_specs=anywhere,
        scratch_shapes=[
            pltpu.VMEM((n, 2, 2, RING, TOK, 2 * DH), bf16),
            pltpu.VMEM((n, RING, 2, TOK, DH), bf16),
            pltpu.VMEM((n, RING, 2 * TOK, DH), bf16),
            pltpu.VMEM((n, RING - 1, 2 * TOK, DH), bf16),
            pltpu.VMEM((n, RING, 8, 2 * TOK), f32),
            pltpu.VMEM((n, RING - 1, 8, 2 * TOK), f32),
            pltpu.VMEM((4 * n, TOK, DH), bf16),
            pltpu.VMEM((n, TOK, DH), bf16),
            pltpu.VMEM(out_weight.shape, bf16),
            pltpu.VMEM(hidden.shape, bf16),
            pltpu.VMEM(hidden.shape, f32),
            pltpu.VMEM((n, RING - 1, 2 * TOK, 1), f32),
            pltpu.VMEM((n, RING - 1, 2 * TOK, 2 * DH), f32),
            pltpu.VMEM(attn_gate.shape, f32),
            pltpu.VMEM(hidden.shape, bf16),
            pltpu.VMEM((n, TOK, 2 * DH), bf16),
            pltpu.VMEM((n, TOK, DH), bf16),
            dma((n, 3)), dma((n, 3)), dma((5,)), dma((n, 2)), dma((n, 2)),
            dma((n, 2, 3)), dma((n, 2, 3)), dma((n, 2, 3)), dma((n, 2, 3)),
            dma((n, 2)), dma((n, 2)), dma((n, 2, 2)), dma((n, 2, 2)), dma((n, 3)), dma((n, 3)), dma((n, 3)), dma((n, 3)),
            dma((n, 3)), dma((n, 3)),
        ],
        compiler_params=pltpu.CompilerParams(
            collective_id=0, has_side_effects=True, vmem_limit_bytes=56 << 20
        ),
        cost_estimate=pl.CostEstimate(flops=15_000_000_000, bytes_accessed=8_000_000, transcendentals=14_000_000),
    )(queries, key_tokens, value_tokens, hidden, out_weight, attn_gate)


def solution(mesh):
    return jax.shard_map(
        on_device,
        mesh=mesh,
        in_specs=(P("ctx", "grp"), P("ctx", "grp"), P("ctx", "grp"), P("ctx", None), P(), P()),
        out_specs=P("ctx", None),
        check_vma=False,
    )
```

```python
import jax
import jax.numpy as jnp
from jax import lax
from jax.experimental import pallas as pl
from jax.experimental.pallas import tpu as pltpu
from jax.sharding import PartitionSpec as P

DH = 128
TOK = 192
HEADS_DEV = 3
RING = 4
SCALE = DH**-0.5 * 1.4426950408889634
NT = (((1,), (1,)), ((), ()))
NN = (((1,), (0,)), ((), ()))
MESH = pl.DeviceIdType.MESH
KV_AXIS = ("y", "z", "z")
Q_AXIS = ("z", "y", "y")
RELAYED = (False, True, True)
HALF = TOK // 2


def kernel(
    q_in, k_in, v_in, hidden_in, w_in, gate_in, out_ref,
    kv, qb, o_send, o_recv, s_send, s_recv, att, a_send, w_buf, hid_buf, proj, top_buf, mix_buf, gate_ref, x_kv_buf, x_q_buf,
    loc_sem, stage_sem, big_sem, x_send, x_recv, kv_send, kv_recv, q_send, q_recv,
    f_send, f_recv, r_send, r_recv, o_ssem, o_rsem, s_ssem, s_rsem, a_ssem, a_rsem,
):
    g = lax.axis_index("grp")
    t = lax.axis_index("ctx")
    core = t % 2
    place = {"xh": t // 32, "y": (t // 8) % 4, "z": (t // 2) % 4, "core": core}
    xh = place["xh"]

    def device(grp=None, **moved):
        at = dict(place, **moved)
        ctx = ((at["xh"] * 4 + at["y"]) * 4 + at["z"]) * 2 + at["core"]
        return (g if grp is None else grp, ctx)

    def ring(axis, step):
        return device(**{axis: (place[axis] + step) % RING})

    sibling = device(core=1 - core)
    x_partner = device(xh=1 - xh)
    x_kinds = (device(grp=1 - g), x_partner, device(grp=1 - g, xh=1 - xh))

    def columns(half, h):
        return pl.ds(pl.multiple_of((half * HEADS_DEV + h) * DH, DH), DH)

    def remote(src, dst, send, recv, to):
        return pltpu.make_async_remote_copy(
            src_ref=src, dst_ref=dst, send_sem=send, recv_sem=recv, device_id=to, device_id_type=MESH
        )

    barrier = pltpu.get_barrier_semaphore()
    peers = [ring(a, s) for a in ("y", "z") for s in (1, 2, 3)] + [sibling, *x_kinds]
    for peer in peers:
        pl.semaphore_signal(barrier, inc=1, device_id=peer, device_id_type=MESH)

    own, stage = [], []
    for h in range(HEADS_DEV):
        cols = columns(xh, h)
        own.append((
            pltpu.make_async_copy(k_in.at[:, cols], kv.at[h, 0, 0, 0, :, pl.ds(0, DH)], loc_sem.at[h, 0]),
            pltpu.make_async_copy(v_in.at[:, cols], kv.at[h, 0, 0, 0, :, pl.ds(DH, DH)], loc_sem.at[h, 1]),
            pltpu.make_async_copy(q_in.at[:, cols], qb.at[h, 0, 0], loc_sem.at[h, 2]),
        ))
        cols = columns(1 - xh, h)
        stage.append((
            pltpu.make_async_copy(k_in.at[:, cols], x_kv_buf.at[h, :, pl.ds(0, DH)], stage_sem.at[h, 0]),
            pltpu.make_async_copy(v_in.at[:, cols], x_kv_buf.at[h, :, pl.ds(DH, DH)], stage_sem.at[h, 1]),
            pltpu.make_async_copy(q_in.at[:, cols], x_q_buf.at[h], stage_sem.at[h, 2]),
        ))
        for copy in (*stage[h], *own[h]):
            copy.start()
    w_copy = pltpu.make_async_copy(w_in, w_buf, big_sem.at[0])
    hid_copy = pltpu.make_async_copy(hidden_in, hid_buf, big_sem.at[1])
    gate_copy = pltpu.make_async_copy(gate_in, gate_ref, big_sem.at[2])

    pl.semaphore_wait(barrier, len(peers))

    sent = []

    def start(copy):
        copy.start()
        sent.append(copy)

    def x_query(h):
        return remote(x_q_buf.at[h], qb.at[h, 0, 1], x_send.at[h, 0], x_recv.at[h, 0], x_partner)

    def x_kv(h):
        return remote(x_kv_buf.at[h], kv.at[h, 0, 1, 0], x_send.at[h, 1], x_recv.at[h, 1], x_partner)

    def kv_copy(h, xr, step):
        slot = RING - step
        return remote(
            kv.at[h, 0, xr, 0], kv.at[h, 0, xr, slot],
            kv_send.at[h, xr, slot - 1], kv_recv.at[h, xr, slot - 1], ring(KV_AXIS[h], step),
        )

    def q_copy(h, xr, step):
        slot = RING - step
        return remote(
            qb.at[h, 0, xr], qb.at[h, slot, xr],
            q_send.at[h, xr, slot - 1], q_recv.at[h, xr, slot - 1], ring(Q_AXIS[h], step),
        )

    def push_queries(h, xr):
        for step in (2, 1, 3):
            start(q_copy(h, xr, step))

    def push_kv(h, xr):
        for step in (1, 3) if RELAYED[h] else (2, 1, 3):
            start(kv_copy(h, xr, step))

    def relay_copy(h, xr, step):
        slot = RING - step
        rows = pl.ds(0 if step == 1 else HALF, HALF)
        n = 0 if step == 1 else 1
        return remote(
            kv.at[h, 0, xr, slot, rows], kv.at[h, 0, xr, 2, rows],
            r_send.at[h, xr, n], r_recv.at[h, xr, n], ring(KV_AXIS[h], step),
        )

    def relay(h, xr):
        for step in (1, 3):
            kv_copy(h, xr, step).wait_recv()
            start(relay_copy(h, xr, step))

    def forward_copy(h, xr):
        return remote(kv.at[h, 0, xr], kv.at[h, 1, xr], f_send.at[h, xr], f_recv.at[h, xr], sibling)

    def gathered(h, xr):
        if RELAYED[h]:
            for step in (1, 3):
                relay_copy(h, xr, step).wait_recv()
        else:
            for step in (1, 2, 3):
                kv_copy(h, xr, step).wait_recv()
        start(forward_copy(h, xr))

    def ready(h, xr):
        forward_copy(h, xr).wait_recv()

    def queries_ready(h):
        for xr in range(2):
            for step in (1, 2, 3):
                q_copy(h, xr, step).wait_recv()

    def o_copies(h, d):
        slot = RING - d
        to = ring(Q_AXIS[h], d)
        return (
            remote(o_send.at[h, d], o_recv.at[h, slot - 1], o_ssem.at[h, slot - 1], o_rsem.at[h, slot - 1], to),
            remote(s_send.at[h, d], s_recv.at[h, slot - 1], s_ssem.at[h, slot - 1], s_rsem.at[h, slot - 1], to),
        )

    def attend(rows, blocks, begin=True, end=True):
        items = [(row, block) for row in rows for block in blocks]
        stacked = {}
        for h, d in rows:
            scaled = qb[h, d].reshape(2 * TOK, DH).astype(jnp.float32) * SCALE
            high = scaled.astype(jnp.bfloat16)
            low = (scaled - high.astype(jnp.float32)).astype(jnp.bfloat16)
            stacked[h, d] = jnp.concatenate([high, low], axis=1)

        def scores(item):
            row, (cs, xr) = item
            keys = kv[row[0], cs, xr, :, :, :DH].reshape(RING * TOK, DH)
            return lax.dot_general(
                stacked[row], jnp.concatenate([keys, keys], axis=1), NT, preferred_element_type=jnp.float32
            )

        state = {}
        if not begin:
            for h, d in rows:
                state[h, d] = (top_buf[h, d - 1], mix_buf[h, d - 1])
        ahead = scores(items[0])
        for n, (row, (cs, xr)) in enumerate(items):
            now = ahead
            if n + 1 < len(items):
                ahead = scores(items[n + 1])
            values = kv[row[0], cs, xr, :, :, DH:].reshape(RING * TOK, DH)
            top = jnp.max(now, axis=1, keepdims=True)
            if row in state:
                top = jnp.maximum(top, state[row][0])
            weights = jnp.exp2(now - top).astype(jnp.bfloat16)
            mixed = lax.dot_general(
                weights, jnp.concatenate([values, jnp.ones_like(values)], axis=1), NN,
                preferred_element_type=jnp.float32,
            )
            if row in state:
                mixed = mixed + state[row][1] * jnp.exp2(state[row][0] - top)
            state[row] = (top, mixed)
        for h, d in rows:
            top, mixed = state[h, d]
            if end:
                mass = mixed[:, DH:]
                o_send[h, d] = (mixed[:, :DH] / mass).astype(jnp.bfloat16)
                s_send[h, d] = jnp.transpose(top + jnp.log2(mass))[:8]
            else:
                top_buf[h, d - 1] = top
                mix_buf[h, d - 1] = mixed
        for h, d in rows:
            if end and d:
                for copy in o_copies(h, d):
                    start(copy)

    def a_copies(h):
        at = (g * 2 + xh) * HEADS_DEV + h
        return [
            remote(att.at[at] if kind == 0 else a_send.at[h], att.at[at], a_ssem.at[h, kind], a_rsem.at[h, kind], x_kinds[kind])
            for kind in range(3)
        ]

    def a_arrivals(h):
        places = ((1 - g) * 2 + xh, g * 2 + 1 - xh, (1 - g) * 2 + 1 - xh)
        return [
            remote(a_send.at[h], att.at[places[kind] * HEADS_DEV + h], a_ssem.at[h, kind], a_rsem.at[h, kind], x_kinds[kind])
            for kind in range(3)
        ]

    def combine(h):
        for d in (1, 2, 3):
            for copy in o_copies(h, d):
                copy.wait_recv()
        sums = [s_send[h, 0]] + [s_recv[h, j] for j in range(3)]
        parts = [o_send[h, 0]] + [o_recv[h, j] for j in range(3)]
        top = jnp.maximum(jnp.maximum(sums[0], sums[1]), jnp.maximum(sums[2], sums[3]))
        shares = [jnp.exp2(s - top) for s in sums]
        total = (shares[0] + shares[1]) + (shares[2] + shares[3])
        whole = None
        for share, part in zip(shares, parts):
            by_row = jnp.transpose(jnp.broadcast_to((share / total)[:1], (DH, 2 * TOK)))
            term = by_row * part.astype(jnp.float32)
            whole = term if whole is None else whole + term
        whole = whole.astype(jnp.bfloat16)
        att[(g * 2 + xh) * HEADS_DEV + h] = whole[:TOK]
        a_send[h] = whole[TOK:]
        for copy in a_copies(h):
            start(copy)

    def project(h, first):
        places = [k * HEADS_DEV + h for k in range(4)]
        rows = jnp.concatenate([att[p] for p in places], axis=1)
        for n in range(0, w_buf.shape[1], 512):
            weight = jnp.concatenate([w_buf[p * DH : (p + 1) * DH, n : n + 512] for p in places], axis=0)
            part = jnp.dot(rows, weight, preferred_element_type=jnp.float32)
            proj[:, n : n + 512] = part if first else proj[:, n : n + 512] + part

    def wait_attended(h):
        for copy in a_arrivals(h):
            copy.wait_recv()

    def remote_rows(h):
        return [(h, d) for d in (1, 3, 2)]

    def start_all(copies):
        for copy in copies:
            start(copy)

    def wait_own(h):
        for copy in own[h]:
            copy.wait()

    def wait_staged(h):
        for copy in stage[h]:
            copy.wait()

    def push_own(h):
        steps = (1, 3) if RELAYED[h] else (2, 1, 3)
        for step in (2, 1, 3):
            start(q_copy(h, 0, step))
            if step in steps:
                start(kv_copy(h, 0, step))

    def partner_queries(h):
        x_query(h).wait_recv()
        push_queries(h, 1)

    def partner_kv(h):
        x_kv(h).wait_recv()
        push_kv(h, 1)

    for h in range(HEADS_DEV):
        wait_staged(h)
        wait_own(h)
    start(x_query(0))
    push_own(0)
    start(x_query(1))
    start(x_kv(0))
    push_own(1)
    partner_queries(0)
    start(x_kv(1))
    partner_queries(1)
    start(x_query(2))
    partner_kv(0)
    start(x_kv(2))
    push_own(2)
    w_copy.start()
    hid_copy.start()
    gate_copy.start()
    relay(1, 0)
    gathered(0, 0)
    queries_ready(0)
    first, second, third = ([(h, d) for d in (1, 3, 2)] for h in range(HEADS_DEV))
    attend(first, [(0, 0)], end=False)
    partner_kv(1)
    ready(0, 0)
    attend(first, [(1, 0)], begin=False, end=False)
    relay(2, 0)
    partner_queries(2)
    partner_kv(2)
    gathered(1, 0)
    queries_ready(1)
    attend(second, [(0, 0)], end=False)
    relay(1, 1)
    ready(1, 0)
    attend(second, [(1, 0)], begin=False, end=False)
    gathered(0, 1)
    attend(first, [(0, 1)], begin=False, end=False)
    relay(2, 1)
    gathered(1, 1)
    ready(0, 1)
    attend(first, [(1, 1)], begin=False)
    gathered(2, 0)
    ready(1, 1)
    attend(second, [(0, 1), (1, 1)], begin=False)
    gathered(2, 1)
    queries_ready(2)
    ready(2, 0)
    attend(third, [(0, 0), (1, 0)], end=False)
    ready(2, 1)
    attend(third, [(0, 1), (1, 1)], begin=False)
    every = [(0, 0), (0, 1), (1, 0), (1, 1)]
    attend([(0, 0), (1, 0)], every)
    combine(0)
    combine(1)
    attend([(2, 0)], every)
    combine(2)
    w_copy.wait()
    hid_copy.wait()
    gate_copy.wait()
    for copy in sent[:-3]:
        copy.wait_send()
    for h in range(HEADS_DEV):
        wait_attended(h)
        project(h, h == 0)
    out_ref[...] = (
        hid_buf[...].astype(jnp.float32) + gate_ref[...].reshape(1, -1) * proj[...]
    ).astype(jnp.bfloat16)
    for copy in sent[-3:]:
        copy.wait_send()


def on_device(queries, key_tokens, value_tokens, hidden, out_weight, attn_gate):
    bf16, f32 = jnp.bfloat16, jnp.float32
    dma = pltpu.SemaphoreType.DMA
    anywhere = pl.BlockSpec(memory_space=pl.ANY)
    n = HEADS_DEV
    return pl.pallas_call(
        kernel,
        out_shape=pltpu.VMEM(hidden.shape, bf16),
        in_specs=[anywhere] * 6,
        out_specs=pl.BlockSpec(memory_space=pltpu.VMEM),
        scratch_shapes=[
            pltpu.VMEM((n, 2, 2, RING, TOK, 2 * DH), bf16),
            pltpu.VMEM((n, RING, 2, TOK, DH), bf16),
            pltpu.VMEM((n, RING, 2 * TOK, DH), bf16),
            pltpu.VMEM((n, RING - 1, 2 * TOK, DH), bf16),
            pltpu.VMEM((n, RING, 8, 2 * TOK), f32),
            pltpu.VMEM((n, RING - 1, 8, 2 * TOK), f32),
            pltpu.VMEM((4 * n, TOK, DH), bf16),
            pltpu.VMEM((n, TOK, DH), bf16),
            pltpu.VMEM(out_weight.shape, bf16),
            pltpu.VMEM(hidden.shape, bf16),
            pltpu.VMEM(hidden.shape, f32),
            pltpu.VMEM((n, RING - 1, 2 * TOK, 1), f32),
            pltpu.VMEM((n, RING - 1, 2 * TOK, 2 * DH), f32),
            pltpu.VMEM(attn_gate.shape, f32),
            pltpu.VMEM((n, TOK, 2 * DH), bf16),
            pltpu.VMEM((n, TOK, DH), bf16),
            dma((n, 3)), dma((n, 3)), dma((3,)), dma((n, 2)), dma((n, 2)),
            dma((n, 2, 3)), dma((n, 2, 3)), dma((n, 2, 3)), dma((n, 2, 3)),
            dma((n, 2)), dma((n, 2)), dma((n, 2, 2)), dma((n, 2, 2)), dma((n, 3)), dma((n, 3)), dma((n, 3)), dma((n, 3)),
            dma((n, 3)), dma((n, 3)),
        ],
        compiler_params=pltpu.CompilerParams(
            collective_id=0, has_side_effects=True, vmem_limit_bytes=56 << 20
        ),
        cost_estimate=pl.CostEstimate(flops=15_000_000_000, bytes_accessed=8_000_000, transcendentals=14_000_000),
    )(queries, key_tokens, value_tokens, hidden, out_weight, attn_gate)


def solution(mesh):
    return jax.shard_map(
        on_device,
        mesh=mesh,
        in_specs=(P("ctx", "grp"), P("ctx", "grp"), P("ctx", "grp"), P("ctx", None), P(), P()),
        out_specs=P("ctx", None),
        check_vma=False,
    )
```

```python
import jax
import jax.numpy as jnp
from jax import lax
from jax.experimental import pallas as pl
from jax.experimental.pallas import tpu as pltpu
from jax.sharding import PartitionSpec as P

DH = 128
TOK = 192
HEADS_DEV = 3
RING = 4
SCALE = DH**-0.5 * 1.4426950408889634
NT = (((1,), (1,)), ((), ()))
NN = (((1,), (0,)), ((), ()))
MESH = pl.DeviceIdType.MESH
KV_AXIS = ("y", "z", "z")
Q_AXIS = ("z", "y", "y")
RELAYED = (False, True, True)
HALF = TOK // 2


def kernel(
    q_in, k_in, v_in, hidden_in, w_in, gate_in, out_ref,
    kv, qb, o_send, o_recv, s_send, s_recv, att, a_send, w_buf, hid_buf, proj, top_buf, mix_buf, gate_ref, x_kv_buf, x_q_buf,
    loc_sem, stage_sem, big_sem, x_send, x_recv, kv_send, kv_recv, q_send, q_recv,
    f_send, f_recv, r_send, r_recv, o_ssem, o_rsem, s_ssem, s_rsem, a_ssem, a_rsem,
):
    g = lax.axis_index("grp")
    t = lax.axis_index("ctx")
    core = t % 2
    place = {"xh": t // 32, "y": (t // 8) % 4, "z": (t // 2) % 4, "core": core}
    xh = place["xh"]

    def device(grp=None, **moved):
        at = dict(place, **moved)
        ctx = ((at["xh"] * 4 + at["y"]) * 4 + at["z"]) * 2 + at["core"]
        return (g if grp is None else grp, ctx)

    def ring(axis, step):
        return device(**{axis: (place[axis] + step) % RING})

    sibling = device(core=1 - core)
    x_partner = device(xh=1 - xh)
    x_kinds = (device(grp=1 - g), x_partner, device(grp=1 - g, xh=1 - xh))

    def columns(half, h):
        return pl.ds(pl.multiple_of((half * HEADS_DEV + h) * DH, DH), DH)

    def remote(src, dst, send, recv, to):
        return pltpu.make_async_remote_copy(
            src_ref=src, dst_ref=dst, send_sem=send, recv_sem=recv, device_id=to, device_id_type=MESH
        )

    barrier = pltpu.get_barrier_semaphore()
    peers = [ring(a, s) for a in ("y", "z") for s in (1, 2, 3)] + [sibling, *x_kinds]
    for peer in peers:
        pl.semaphore_signal(barrier, inc=1, device_id=peer, device_id_type=MESH)

    own, stage = [], []
    for h in range(HEADS_DEV):
        cols = columns(xh, h)
        own.append((
            pltpu.make_async_copy(k_in.at[:, cols], kv.at[h, 0, 0, 0, :, pl.ds(0, DH)], loc_sem.at[h, 0]),
            pltpu.make_async_copy(v_in.at[:, cols], kv.at[h, 0, 0, 0, :, pl.ds(DH, DH)], loc_sem.at[h, 1]),
            pltpu.make_async_copy(q_in.at[:, cols], qb.at[h, 0, 0], loc_sem.at[h, 2]),
        ))
        cols = columns(1 - xh, h)
        stage.append((
            pltpu.make_async_copy(k_in.at[:, cols], x_kv_buf.at[h, :, pl.ds(0, DH)], stage_sem.at[h, 0]),
            pltpu.make_async_copy(v_in.at[:, cols], x_kv_buf.at[h, :, pl.ds(DH, DH)], stage_sem.at[h, 1]),
            pltpu.make_async_copy(q_in.at[:, cols], x_q_buf.at[h], stage_sem.at[h, 2]),
        ))
        for copy in (*stage[h], *own[h]):
            copy.start()
    w_copy = pltpu.make_async_copy(w_in, w_buf, big_sem.at[0])
    hid_copy = pltpu.make_async_copy(hidden_in, hid_buf, big_sem.at[1])
    gate_copy = pltpu.make_async_copy(gate_in, gate_ref, big_sem.at[2])

    pl.semaphore_wait(barrier, len(peers))

    sent = []

    def start(copy):
        copy.start()
        sent.append(copy)

    def x_query(h):
        return remote(x_q_buf.at[h], qb.at[h, 0, 1], x_send.at[h, 0], x_recv.at[h, 0], x_partner)

    def x_kv(h):
        return remote(x_kv_buf.at[h], kv.at[h, 0, 1, 0], x_send.at[h, 1], x_recv.at[h, 1], x_partner)

    def kv_copy(h, xr, step):
        slot = RING - step
        return remote(
            kv.at[h, 0, xr, 0], kv.at[h, 0, xr, slot],
            kv_send.at[h, xr, slot - 1], kv_recv.at[h, xr, slot - 1], ring(KV_AXIS[h], step),
        )

    def q_copy(h, xr, step):
        slot = RING - step
        return remote(
            qb.at[h, 0, xr], qb.at[h, slot, xr],
            q_send.at[h, xr, slot - 1], q_recv.at[h, xr, slot - 1], ring(Q_AXIS[h], step),
        )

    def push_queries(h, xr):
        for step in (2, 1, 3):
            start(q_copy(h, xr, step))

    def push_kv(h, xr):
        for step in (1, 3) if RELAYED[h] else (2, 1, 3):
            start(kv_copy(h, xr, step))

    def relay_copy(h, xr, step):
        slot = RING - step
        rows = pl.ds(0 if step == 1 else HALF, HALF)
        n = 0 if step == 1 else 1
        return remote(
            kv.at[h, 0, xr, slot, rows], kv.at[h, 0, xr, 2, rows],
            r_send.at[h, xr, n], r_recv.at[h, xr, n], ring(KV_AXIS[h], step),
        )

    def relay(h, xr):
        for step in (1, 3):
            kv_copy(h, xr, step).wait_recv()
            start(relay_copy(h, xr, step))

    def forward_copy(h, xr):
        return remote(kv.at[h, 0, xr], kv.at[h, 1, xr], f_send.at[h, xr], f_recv.at[h, xr], sibling)

    def gathered(h, xr):
        if RELAYED[h]:
            for step in (1, 3):
                relay_copy(h, xr, step).wait_recv()
        else:
            for step in (1, 2, 3):
                kv_copy(h, xr, step).wait_recv()
        start(forward_copy(h, xr))

    def ready(h, xr):
        forward_copy(h, xr).wait_recv()

    def queries_ready(h):
        for xr in range(2):
            for step in (1, 2, 3):
                q_copy(h, xr, step).wait_recv()

    def o_copies(h, d):
        slot = RING - d
        to = ring(Q_AXIS[h], d)
        return (
            remote(o_send.at[h, d], o_recv.at[h, slot - 1], o_ssem.at[h, slot - 1], o_rsem.at[h, slot - 1], to),
            remote(s_send.at[h, d], s_recv.at[h, slot - 1], s_ssem.at[h, slot - 1], s_rsem.at[h, slot - 1], to),
        )

    def attend(rows, blocks, begin=True, end=True):
        items = [(row, block) for row in rows for block in blocks]
        stacked = {}
        for h, d in rows:
            scaled = qb[h, d].reshape(2 * TOK, DH).astype(jnp.float32) * SCALE
            high = scaled.astype(jnp.bfloat16)
            low = (scaled - high.astype(jnp.float32)).astype(jnp.bfloat16)
            stacked[h, d] = jnp.concatenate([high, low], axis=1)

        def scores(item):
            row, (cs, xr) = item
            keys = kv[row[0], cs, xr, :, :, :DH].reshape(RING * TOK, DH)
            return lax.dot_general(
                stacked[row], jnp.concatenate([keys, keys], axis=1), NT, preferred_element_type=jnp.float32
            )

        state = {}
        if not begin:
            for h, d in rows:
                state[h, d] = (top_buf[h, d - 1], mix_buf[h, d - 1])
        ahead = scores(items[0])
        for n, (row, (cs, xr)) in enumerate(items):
            now = ahead
            if n + 1 < len(items):
                ahead = scores(items[n + 1])
            values = kv[row[0], cs, xr, :, :, DH:].reshape(RING * TOK, DH)
            top = jnp.max(now, axis=1, keepdims=True)
            if row in state:
                top = jnp.maximum(top, state[row][0])
            weights = jnp.exp2(now - top).astype(jnp.bfloat16)
            mixed = lax.dot_general(
                weights, jnp.concatenate([values, jnp.ones_like(values)], axis=1), NN,
                preferred_element_type=jnp.float32,
            )
            if row in state:
                mixed = mixed + state[row][1] * jnp.exp2(state[row][0] - top)
            state[row] = (top, mixed)
        for h, d in rows:
            top, mixed = state[h, d]
            if end:
                mass = mixed[:, DH:]
                o_send[h, d] = (mixed[:, :DH] / mass).astype(jnp.bfloat16)
                s_send[h, d] = jnp.transpose(top + jnp.log2(mass))[:8]
            else:
                top_buf[h, d - 1] = top
                mix_buf[h, d - 1] = mixed
        for h, d in rows:
            if end and d:
                for copy in o_copies(h, d):
                    start(copy)

    def a_copies(h):
        at = (g * 2 + xh) * HEADS_DEV + h
        return [
            remote(att.at[at] if kind == 0 else a_send.at[h], att.at[at], a_ssem.at[h, kind], a_rsem.at[h, kind], x_kinds[kind])
            for kind in range(3)
        ]

    def a_arrivals(h):
        places = ((1 - g) * 2 + xh, g * 2 + 1 - xh, (1 - g) * 2 + 1 - xh)
        return [
            remote(a_send.at[h], att.at[places[kind] * HEADS_DEV + h], a_ssem.at[h, kind], a_rsem.at[h, kind], x_kinds[kind])
            for kind in range(3)
        ]

    def combine(h):
        for d in (1, 2, 3):
            for copy in o_copies(h, d):
                copy.wait_recv()
        sums = [s_send[h, 0]] + [s_recv[h, j] for j in range(3)]
        parts = [o_send[h, 0]] + [o_recv[h, j] for j in range(3)]
        top = jnp.maximum(jnp.maximum(sums[0], sums[1]), jnp.maximum(sums[2], sums[3]))
        shares = [jnp.exp2(s - top) for s in sums]
        total = (shares[0] + shares[1]) + (shares[2] + shares[3])
        whole = None
        for share, part in zip(shares, parts):
            by_row = jnp.transpose(jnp.broadcast_to((share / total)[:1], (DH, 2 * TOK)))
            term = by_row * part.astype(jnp.float32)
            whole = term if whole is None else whole + term
        whole = whole.astype(jnp.bfloat16)
        att[(g * 2 + xh) * HEADS_DEV + h] = whole[:TOK]
        a_send[h] = whole[TOK:]
        copies = a_copies(h)
        for kind in (1, 2, 0):
            start(copies[kind])

    def project(h, first):
        places = [k * HEADS_DEV + h for k in range(4)]
        rows = jnp.concatenate([att[p] for p in places], axis=1)
        for n in range(0, w_buf.shape[1], 512):
            weight = jnp.concatenate([w_buf[p * DH : (p + 1) * DH, n : n + 512] for p in places], axis=0)
            part = jnp.dot(rows, weight, preferred_element_type=jnp.float32)
            proj[:, n : n + 512] = part if first else proj[:, n : n + 512] + part

    def wait_attended(h):
        for copy in a_arrivals(h):
            copy.wait_recv()

    def remote_rows(h):
        return [(h, d) for d in (1, 3, 2)]

    def start_all(copies):
        for copy in copies:
            start(copy)

    def wait_own(h):
        for copy in own[h]:
            copy.wait()

    def wait_staged(h):
        for copy in stage[h]:
            copy.wait()

    def push_own(h):
        steps = (1, 3) if RELAYED[h] else (2, 1, 3)
        for step in (2, 1, 3):
            start(q_copy(h, 0, step))
            if step in steps:
                start(kv_copy(h, 0, step))

    def partner_queries(h):
        x_query(h).wait_recv()
        push_queries(h, 1)

    def partner_kv(h):
        x_kv(h).wait_recv()
        push_kv(h, 1)

    for h in range(HEADS_DEV):
        wait_staged(h)
        wait_own(h)
    start(x_query(0))
    push_own(0)
    start(x_query(1))
    start(x_kv(0))
    push_own(1)
    partner_queries(0)
    start(x_kv(1))
    partner_queries(1)
    start(x_query(2))
    partner_kv(0)
    start(x_kv(2))
    push_own(2)
    w_copy.start()
    hid_copy.start()
    gate_copy.start()
    relay(1, 0)
    gathered(0, 0)
    queries_ready(0)
    first, second, third = ([(h, d) for d in (1, 3, 2)] for h in range(HEADS_DEV))
    attend(first, [(0, 0)], end=False)
    partner_kv(1)
    ready(0, 0)
    attend(first, [(1, 0)], begin=False, end=False)
    relay(2, 0)
    partner_queries(2)
    partner_kv(2)
    gathered(1, 0)
    queries_ready(1)
    attend(second, [(0, 0)], end=False)
    relay(1, 1)
    ready(1, 0)
    attend(second, [(1, 0)], begin=False, end=False)
    gathered(0, 1)
    attend(first, [(0, 1)], begin=False, end=False)
    relay(2, 1)
    gathered(1, 1)
    ready(0, 1)
    attend(first, [(1, 1)], begin=False)
    gathered(2, 0)
    ready(1, 1)
    attend(second, [(0, 1), (1, 1)], begin=False)
    gathered(2, 1)
    queries_ready(2)
    ready(2, 0)
    attend(third, [(0, 0), (1, 0)], end=False)
    ready(2, 1)
    attend(third, [(0, 1), (1, 1)], begin=False)
    every = [(0, 0), (0, 1), (1, 0), (1, 1)]
    for h in range(HEADS_DEV):
        attend([(h, 0)], every)
        combine(h)
    w_copy.wait()
    hid_copy.wait()
    gate_copy.wait()
    for copy in sent[:-3]:
        copy.wait_send()
    for h in range(HEADS_DEV):
        wait_attended(h)
        project(h, h == 0)
    out_ref[...] = (
        hid_buf[...].astype(jnp.float32) + gate_ref[...].reshape(1, -1) * proj[...]
    ).astype(jnp.bfloat16)
    for copy in sent[-3:]:
        copy.wait_send()


def on_device(queries, key_tokens, value_tokens, hidden, out_weight, attn_gate):
    bf16, f32 = jnp.bfloat16, jnp.float32
    dma = pltpu.SemaphoreType.DMA
    anywhere = pl.BlockSpec(memory_space=pl.ANY)
    n = HEADS_DEV
    return pl.pallas_call(
        kernel,
        out_shape=pltpu.VMEM(hidden.shape, bf16),
        in_specs=[anywhere] * 6,
        out_specs=pl.BlockSpec(memory_space=pltpu.VMEM),
        scratch_shapes=[
            pltpu.VMEM((n, 2, 2, RING, TOK, 2 * DH), bf16),
            pltpu.VMEM((n, RING, 2, TOK, DH), bf16),
            pltpu.VMEM((n, RING, 2 * TOK, DH), bf16),
            pltpu.VMEM((n, RING - 1, 2 * TOK, DH), bf16),
            pltpu.VMEM((n, RING, 8, 2 * TOK), f32),
            pltpu.VMEM((n, RING - 1, 8, 2 * TOK), f32),
            pltpu.VMEM((4 * n, TOK, DH), bf16),
            pltpu.VMEM((n, TOK, DH), bf16),
            pltpu.VMEM(out_weight.shape, bf16),
            pltpu.VMEM(hidden.shape, bf16),
            pltpu.VMEM(hidden.shape, f32),
            pltpu.VMEM((n, RING - 1, 2 * TOK, 1), f32),
            pltpu.VMEM((n, RING - 1, 2 * TOK, 2 * DH), f32),
            pltpu.VMEM(attn_gate.shape, f32),
            pltpu.VMEM((n, TOK, 2 * DH), bf16),
            pltpu.VMEM((n, TOK, DH), bf16),
            dma((n, 3)), dma((n, 3)), dma((3,)), dma((n, 2)), dma((n, 2)),
            dma((n, 2, 3)), dma((n, 2, 3)), dma((n, 2, 3)), dma((n, 2, 3)),
            dma((n, 2)), dma((n, 2)), dma((n, 2, 2)), dma((n, 2, 2)), dma((n, 3)), dma((n, 3)), dma((n, 3)), dma((n, 3)),
            dma((n, 3)), dma((n, 3)),
        ],
        compiler_params=pltpu.CompilerParams(
            collective_id=0, has_side_effects=True, vmem_limit_bytes=56 << 20
        ),
        cost_estimate=pl.CostEstimate(flops=15_000_000_000, bytes_accessed=8_000_000, transcendentals=14_000_000),
    )(queries, key_tokens, value_tokens, hidden, out_weight, attn_gate)


def solution(mesh):
    return jax.shard_map(
        on_device,
        mesh=mesh,
        in_specs=(P("ctx", "grp"), P("ctx", "grp"), P("ctx", "grp"), P("ctx", None), P(), P()),
        out_specs=P("ctx", None),
        check_vma=False,
    )
```

```python
import jax
import jax.numpy as jnp
from jax import lax
from jax.experimental import pallas as pl
from jax.experimental.pallas import tpu as pltpu
from jax.sharding import PartitionSpec as P

DH = 128
TOK = 192
HEADS_DEV = 3
RING = 4
SCALE = DH**-0.5 * 1.4426950408889634
NT = (((1,), (1,)), ((), ()))
NN = (((1,), (0,)), ((), ()))
MESH = pl.DeviceIdType.MESH
KV_AXIS = ("y", "z", "z")
Q_AXIS = ("z", "y", "y")
RELAYED = (False, True, True)
HALF = TOK // 2


def kernel(
    q_in, k_in, v_in, hidden_in, w_in, gate_in, out_ref,
    kv, qb, o_send, o_recv, s_send, s_recv, att, a_send, w_buf, hid_buf, proj, top_buf, mix_buf, gate_ref, x_kv_buf, x_q_buf,
    loc_sem, stage_sem, big_sem, x_send, x_recv, kv_send, kv_recv, q_send, q_recv,
    f_send, f_recv, r_send, r_recv, o_ssem, o_rsem, s_ssem, s_rsem, a_ssem, a_rsem,
):
    g = lax.axis_index("grp")
    t = lax.axis_index("ctx")
    core = t % 2
    place = {"xh": t // 32, "y": (t // 8) % 4, "z": (t // 2) % 4, "core": core}
    xh = place["xh"]

    def device(grp=None, **moved):
        at = dict(place, **moved)
        ctx = ((at["xh"] * 4 + at["y"]) * 4 + at["z"]) * 2 + at["core"]
        return (g if grp is None else grp, ctx)

    def ring(axis, step):
        return device(**{axis: (place[axis] + step) % RING})

    sibling = device(core=1 - core)
    x_partner = device(xh=1 - xh)
    x_kinds = (device(grp=1 - g), x_partner, device(grp=1 - g, xh=1 - xh))

    def columns(half, h):
        return pl.ds(pl.multiple_of((half * HEADS_DEV + h) * DH, DH), DH)

    def remote(src, dst, send, recv, to):
        return pltpu.make_async_remote_copy(
            src_ref=src, dst_ref=dst, send_sem=send, recv_sem=recv, device_id=to, device_id_type=MESH
        )

    barrier = pltpu.get_barrier_semaphore()
    peers = [ring(a, s) for a in ("y", "z") for s in (1, 2, 3)] + [sibling, *x_kinds]
    for peer in peers:
        pl.semaphore_signal(barrier, inc=1, device_id=peer, device_id_type=MESH)

    own, stage = [], []
    for h in range(HEADS_DEV):
        cols = columns(xh, h)
        own.append((
            pltpu.make_async_copy(k_in.at[:, cols], kv.at[h, 0, 0, 0, :, pl.ds(0, DH)], loc_sem.at[h, 0]),
            pltpu.make_async_copy(v_in.at[:, cols], kv.at[h, 0, 0, 0, :, pl.ds(DH, DH)], loc_sem.at[h, 1]),
            pltpu.make_async_copy(q_in.at[:, cols], qb.at[h, 0, 0], loc_sem.at[h, 2]),
        ))
        cols = columns(1 - xh, h)
        stage.append((
            pltpu.make_async_copy(k_in.at[:, cols], x_kv_buf.at[h, :, pl.ds(0, DH)], stage_sem.at[h, 0]),
            pltpu.make_async_copy(v_in.at[:, cols], x_kv_buf.at[h, :, pl.ds(DH, DH)], stage_sem.at[h, 1]),
            pltpu.make_async_copy(q_in.at[:, cols], x_q_buf.at[h], stage_sem.at[h, 2]),
        ))
        for copy in (*stage[h], *own[h]):
            copy.start()
    w_copy = pltpu.make_async_copy(w_in, w_buf, big_sem.at[0])
    hid_copy = pltpu.make_async_copy(hidden_in, hid_buf, big_sem.at[1])
    gate_copy = pltpu.make_async_copy(gate_in, gate_ref, big_sem.at[2])

    pl.semaphore_wait(barrier, len(peers))

    sent = []

    def start(copy):
        copy.start()
        sent.append(copy)

    def x_query(h):
        return remote(x_q_buf.at[h], qb.at[h, 0, 1], x_send.at[h, 0], x_recv.at[h, 0], x_partner)

    def x_kv(h):
        return remote(x_kv_buf.at[h], kv.at[h, 0, 1, 0], x_send.at[h, 1], x_recv.at[h, 1], x_partner)

    def kv_copy(h, xr, step):
        slot = RING - step
        return remote(
            kv.at[h, 0, xr, 0], kv.at[h, 0, xr, slot],
            kv_send.at[h, xr, slot - 1], kv_recv.at[h, xr, slot - 1], ring(KV_AXIS[h], step),
        )

    def q_copy(h, xr, step):
        slot = RING - step
        return remote(
            qb.at[h, 0, xr], qb.at[h, slot, xr],
            q_send.at[h, xr, slot - 1], q_recv.at[h, xr, slot - 1], ring(Q_AXIS[h], step),
        )

    def push_queries(h, xr):
        for step in (2, 1, 3):
            start(q_copy(h, xr, step))

    def push_kv(h, xr):
        for step in (1, 3) if RELAYED[h] else (2, 1, 3):
            start(kv_copy(h, xr, step))

    def relay_copy(h, xr, step):
        slot = RING - step
        rows = pl.ds(0 if step == 1 else HALF, HALF)
        n = 0 if step == 1 else 1
        return remote(
            kv.at[h, 0, xr, slot, rows], kv.at[h, 0, xr, 2, rows],
            r_send.at[h, xr, n], r_recv.at[h, xr, n], ring(KV_AXIS[h], step),
        )

    def relay(h, xr):
        for step in (1, 3):
            kv_copy(h, xr, step).wait_recv()
            start(relay_copy(h, xr, step))

    def forward_copy(h, xr):
        return remote(kv.at[h, 0, xr], kv.at[h, 1, xr], f_send.at[h, xr], f_recv.at[h, xr], sibling)

    def gathered(h, xr):
        if RELAYED[h]:
            for step in (1, 3):
                relay_copy(h, xr, step).wait_recv()
        else:
            for step in (1, 2, 3):
                kv_copy(h, xr, step).wait_recv()
        start(forward_copy(h, xr))

    def ready(h, xr):
        forward_copy(h, xr).wait_recv()

    def queries_ready(h):
        for xr in range(2):
            for step in (1, 2, 3):
                q_copy(h, xr, step).wait_recv()

    def o_copies(h, d):
        slot = RING - d
        to = ring(Q_AXIS[h], d)
        return (
            remote(o_send.at[h, d], o_recv.at[h, slot - 1], o_ssem.at[h, slot - 1], o_rsem.at[h, slot - 1], to),
            remote(s_send.at[h, d], s_recv.at[h, slot - 1], s_ssem.at[h, slot - 1], s_rsem.at[h, slot - 1], to),
        )

    def attend(rows, blocks, begin=True, end=True):
        items = [(row, block) for row in rows for block in blocks]
        stacked = {}
        for h, d in rows:
            scaled = qb[h, d].reshape(2 * TOK, DH).astype(jnp.float32) * SCALE
            high = scaled.astype(jnp.bfloat16)
            low = (scaled - high.astype(jnp.float32)).astype(jnp.bfloat16)
            stacked[h, d] = jnp.concatenate([high, low], axis=1)

        def scores(item):
            row, (cs, xr) = item
            keys = kv[row[0], cs, xr, :, :, :DH].reshape(RING * TOK, DH)
            return lax.dot_general(
                stacked[row], jnp.concatenate([keys, keys], axis=1), NT, preferred_element_type=jnp.float32
            )

        state = {}
        if not begin:
            for h, d in rows:
                state[h, d] = (top_buf[h, d - 1], mix_buf[h, d - 1])
        ahead = scores(items[0])
        for n, (row, (cs, xr)) in enumerate(items):
            now = ahead
            if n + 1 < len(items):
                ahead = scores(items[n + 1])
            values = kv[row[0], cs, xr, :, :, DH:].reshape(RING * TOK, DH)
            top = jnp.max(now, axis=1, keepdims=True)
            if row in state:
                top = jnp.maximum(top, state[row][0])
            weights = jnp.exp2(now - top).astype(jnp.bfloat16)
            mixed = lax.dot_general(
                weights, jnp.concatenate([values, jnp.ones_like(values)], axis=1), NN,
                preferred_element_type=jnp.float32,
            )
            if row in state:
                mixed = mixed + state[row][1] * jnp.exp2(state[row][0] - top)
            state[row] = (top, mixed)
        for h, d in rows:
            top, mixed = state[h, d]
            if end:
                mass = mixed[:, DH:]
                o_send[h, d] = (mixed[:, :DH] / mass).astype(jnp.bfloat16)
                s_send[h, d] = jnp.transpose(top + jnp.log2(mass))[:8]
            else:
                top_buf[h, d - 1] = top
                mix_buf[h, d - 1] = mixed
        for h, d in sorted(rows, key=lambda row: row[1] != 2):
            if end and d:
                for copy in o_copies(h, d):
                    start(copy)

    def a_copies(h):
        at = (g * 2 + xh) * HEADS_DEV + h
        return [
            remote(att.at[at] if kind == 0 else a_send.at[h], att.at[at], a_ssem.at[h, kind], a_rsem.at[h, kind], x_kinds[kind])
            for kind in range(3)
        ]

    def a_arrivals(h):
        places = ((1 - g) * 2 + xh, g * 2 + 1 - xh, (1 - g) * 2 + 1 - xh)
        return [
            remote(a_send.at[h], att.at[places[kind] * HEADS_DEV + h], a_ssem.at[h, kind], a_rsem.at[h, kind], x_kinds[kind])
            for kind in range(3)
        ]

    def combine(h):
        for d in (1, 2, 3):
            for copy in o_copies(h, d):
                copy.wait_recv()
        sums = [s_send[h, 0]] + [s_recv[h, j] for j in range(3)]
        parts = [o_send[h, 0]] + [o_recv[h, j] for j in range(3)]
        top = jnp.maximum(jnp.maximum(sums[0], sums[1]), jnp.maximum(sums[2], sums[3]))
        shares = [jnp.exp2(s - top) for s in sums]
        total = (shares[0] + shares[1]) + (shares[2] + shares[3])
        whole = None
        for share, part in zip(shares, parts):
            by_row = jnp.transpose(jnp.broadcast_to((share / total)[:1], (DH, 2 * TOK)))
            term = by_row * part.astype(jnp.float32)
            whole = term if whole is None else whole + term
        whole = whole.astype(jnp.bfloat16)
        att[(g * 2 + xh) * HEADS_DEV + h] = whole[:TOK]
        a_send[h] = whole[TOK:]
        copies = a_copies(h)
        for kind in (1, 2, 0):
            start(copies[kind])

    def project(h, first):
        places = [k * HEADS_DEV + h for k in range(4)]
        rows = jnp.concatenate([att[p] for p in places], axis=1)
        for n in range(0, w_buf.shape[1], 512):
            weight = jnp.concatenate([w_buf[p * DH : (p + 1) * DH, n : n + 512] for p in places], axis=0)
            part = jnp.dot(rows, weight, preferred_element_type=jnp.float32)
            proj[:, n : n + 512] = part if first else proj[:, n : n + 512] + part

    def wait_attended(h):
        for copy in a_arrivals(h):
            copy.wait_recv()

    def remote_rows(h):
        return [(h, d) for d in (1, 3, 2)]

    def start_all(copies):
        for copy in copies:
            start(copy)

    def wait_own(h):
        for copy in own[h]:
            copy.wait()

    def wait_staged(h):
        for copy in stage[h]:
            copy.wait()

    def push_own(h):
        steps = (1, 3) if RELAYED[h] else (2, 1, 3)
        for step in (2, 1, 3):
            start(q_copy(h, 0, step))
            if step in steps:
                start(kv_copy(h, 0, step))

    def partner_queries(h):
        x_query(h).wait_recv()
        push_queries(h, 1)

    def partner_kv(h):
        x_kv(h).wait_recv()
        push_kv(h, 1)

    for h in range(HEADS_DEV):
        wait_staged(h)
        wait_own(h)
    start(x_query(0))
    push_own(0)
    start(x_query(1))
    start(x_kv(0))
    push_own(1)
    partner_queries(0)
    start(x_kv(1))
    partner_queries(1)
    start(x_query(2))
    partner_kv(0)
    start(x_kv(2))
    push_own(2)
    w_copy.start()
    hid_copy.start()
    gate_copy.start()
    relay(1, 0)
    gathered(0, 0)
    queries_ready(0)
    first, second, third = ([(h, d) for d in (1, 3, 2)] for h in range(HEADS_DEV))
    attend(first, [(0, 0)], end=False)
    partner_kv(1)
    ready(0, 0)
    attend(first, [(1, 0)], begin=False, end=False)
    relay(2, 0)
    partner_queries(2)
    partner_kv(2)
    gathered(1, 0)
    queries_ready(1)
    attend(second, [(0, 0)], end=False)
    relay(1, 1)
    ready(1, 0)
    attend(second, [(1, 0)], begin=False, end=False)
    gathered(0, 1)
    attend(first, [(0, 1)], begin=False, end=False)
    relay(2, 1)
    gathered(1, 1)
    ready(0, 1)
    attend(first, [(1, 1)], begin=False)
    gathered(2, 0)
    ready(1, 1)
    attend(second, [(0, 1), (1, 1)], begin=False)
    gathered(2, 1)
    queries_ready(2)
    ready(2, 0)
    attend(third, [(0, 0), (1, 0)], end=False)
    ready(2, 1)
    attend(third, [(0, 1), (1, 1)], begin=False)
    every = [(0, 0), (0, 1), (1, 0), (1, 1)]
    for h in range(HEADS_DEV):
        attend([(h, 0)], every)
        combine(h)
    w_copy.wait()
    hid_copy.wait()
    gate_copy.wait()
    for copy in sent[:-3]:
        copy.wait_send()
    for h in range(HEADS_DEV):
        wait_attended(h)
        project(h, h == 0)
    out_ref[...] = (
        hid_buf[...].astype(jnp.float32) + gate_ref[...].reshape(1, -1) * proj[...]
    ).astype(jnp.bfloat16)
    for copy in sent[-3:]:
        copy.wait_send()


def on_device(queries, key_tokens, value_tokens, hidden, out_weight, attn_gate):
    bf16, f32 = jnp.bfloat16, jnp.float32
    dma = pltpu.SemaphoreType.DMA
    anywhere = pl.BlockSpec(memory_space=pl.ANY)
    n = HEADS_DEV
    return pl.pallas_call(
        kernel,
        out_shape=pltpu.VMEM(hidden.shape, bf16),
        in_specs=[anywhere] * 6,
        out_specs=pl.BlockSpec(memory_space=pltpu.VMEM),
        scratch_shapes=[
            pltpu.VMEM((n, 2, 2, RING, TOK, 2 * DH), bf16),
            pltpu.VMEM((n, RING, 2, TOK, DH), bf16),
            pltpu.VMEM((n, RING, 2 * TOK, DH), bf16),
            pltpu.VMEM((n, RING - 1, 2 * TOK, DH), bf16),
            pltpu.VMEM((n, RING, 8, 2 * TOK), f32),
            pltpu.VMEM((n, RING - 1, 8, 2 * TOK), f32),
            pltpu.VMEM((4 * n, TOK, DH), bf16),
            pltpu.VMEM((n, TOK, DH), bf16),
            pltpu.VMEM(out_weight.shape, bf16),
            pltpu.VMEM(hidden.shape, bf16),
            pltpu.VMEM(hidden.shape, f32),
            pltpu.VMEM((n, RING - 1, 2 * TOK, 1), f32),
            pltpu.VMEM((n, RING - 1, 2 * TOK, 2 * DH), f32),
            pltpu.VMEM(attn_gate.shape, f32),
            pltpu.VMEM((n, TOK, 2 * DH), bf16),
            pltpu.VMEM((n, TOK, DH), bf16),
            dma((n, 3)), dma((n, 3)), dma((3,)), dma((n, 2)), dma((n, 2)),
            dma((n, 2, 3)), dma((n, 2, 3)), dma((n, 2, 3)), dma((n, 2, 3)),
            dma((n, 2)), dma((n, 2)), dma((n, 2, 2)), dma((n, 2, 2)), dma((n, 3)), dma((n, 3)), dma((n, 3)), dma((n, 3)),
            dma((n, 3)), dma((n, 3)),
        ],
        compiler_params=pltpu.CompilerParams(
            collective_id=0, has_side_effects=True, vmem_limit_bytes=56 << 20
        ),
        cost_estimate=pl.CostEstimate(flops=15_000_000_000, bytes_accessed=8_000_000, transcendentals=14_000_000),
    )(queries, key_tokens, value_tokens, hidden, out_weight, attn_gate)


def solution(mesh):
    return jax.shard_map(
        on_device,
        mesh=mesh,
        in_specs=(P("ctx", "grp"), P("ctx", "grp"), P("ctx", "grp"), P("ctx", None), P(), P()),
        out_specs=P("ctx", None),
        check_vma=False,
    )
```
